32 devices in a mesh: gas: 8 (over z, y), space: 4 (over x, core).
Axes of the slice: x: 2, y: 2, z: 4, core: 2. Of those that a mesh axis runs over, the one named last changes fastest.
Arguments:
- particle_amount: bfloat16 [1024, 256, 8, 128], P('gas', 'space'), may hold values from 0 to 1
- section_opacity: bfloat16 [1024, 16], P('gas'), may hold values from 0.0009994507 to 0.0099487305
- species_opacity_factor: float32 [16], replicated, may hold values from 0.05 to 0.5
- absorber_molefraction: float32 [256, 8, 128], P('space'), may hold values from 0 to 1
- scaled_heat_level: float32 [256, 8, 128], P('space'), may hold values from 0.24 to 1.68
- wall_touching_flag: int32 [256, 8, 128], P('space'), may hold values 0 or 1
- fraction_polynomial: float32 [16, 3], replicated, may hold values from 0.05 to 1.35
Outputs:
- divergence: float32 [256, 8, 128], P('space')
- average_radiative_loss: float32 [], replicated
The draws below stay inside these ranges and needn't reach their ends.
All inputs are finite; a program needn't handle non-finite values. No bound on the sum of `wall_touching_flag` on one device may be relied on, other than what follows from the above.
Results may differ from the reference program's by a relative error of at most 0.0003.
Values sent between devices are 32-bit elements; how exact they have to be, the bound alone decides.
A program may use at most 64 MiB of HBM per device.

```python
import math
import jax
import jax.numpy as jnp

SECTIONS = 1024
GASES = 16
NY = 8
NZ = 128
SWEEPS = 6
NX = 256


def draw_particle_amount(key, part):
    load_key = jax.random.fold_in(key, 11)
    section_key = jax.random.fold_in(key, 12)
    rough_key = jax.random.fold_in(key, 13)
    load = jnp.exp(jax.random.uniform(load_key, (1, NX, NY, NZ), jnp.float32, minval=math.log(0.05), maxval=0.0))
    section = jnp.exp(jax.random.uniform(section_key, (SECTIONS, 1, 1, 1), jnp.float32, minval=math.log(0.1), maxval=0.0))
    rough = jax.random.uniform(rough_key, (SECTIONS, NX, NY, NZ), jnp.float32)
    return (load * section * rough).astype(jnp.bfloat16)


def draw_scaled_heat_level(key, part):
    position = jax.lax.broadcasted_iota(jnp.float32, (NX, NY, NZ), 0)
    ramped = 0.4 + 0.8 * position / (NX - 1)
    factor = jax.random.uniform(key, (NX, NY, NZ), jnp.float32, minval=0.75, maxval=1.25)
    return ramped * factor


def draw_fraction_polynomial(key, part):
    gas_place = jax.lax.broadcasted_iota(jnp.float32, (GASES, 3), 0)
    order_place = jax.lax.broadcasted_iota(jnp.float32, (GASES, 3), 1)
    factor = jax.random.uniform(key, (GASES, 3), jnp.float32, minval=0.5, maxval=1.5)
    return 0.3 * (1.0 + 2.0 * gas_place / (GASES - 1)) * factor / (order_place + 1.0)


def place_ends(array, own_key, smallest, high):
    extent = array.shape
    place = [jax.random.randint(jax.random.fold_in(own_key, axis), (), 0, extent[axis]) for axis in range(len(extent))]
    array = array.at[tuple(place)].set(smallest)
    longest = extent.index(max(extent))
    place[longest] = (place[longest] + 1) % extent[longest]
    return array.at[tuple(place)].set(high)


def shard_levels(own_key, extent, shards, least, top_value):
    loudness, own = 1.0, jax.random.fold_in(own_key, 6)
    for axis_at, blocks in shards:
        steps = jnp.exp(jax.random.uniform(jax.random.fold_in(own, axis_at), (blocks,), jnp.float32, least / len(shards), top_value / len(shards)))
        loudness = loudness * jnp.repeat(steps, extent[axis_at] // blocks).reshape([-1 if axis == axis_at else 1 for axis in range(len(extent))])
    return loudness


def setup_inputs(seed: int = 0) -> dict:
    seeds = jax.random.split(jax.random.key(seed), 8)
    return {
        "particle_amount": draw_particle_amount(jax.random.fold_in(seeds[7], 71), 0),
        "section_opacity": jnp.clip(jnp.exp(math.log(0.0099487305) - 2.2979944 * jax.random.uniform(seeds[1], (SECTIONS, GASES), jnp.float32) ** shard_levels(seeds[1], (SECTIONS, GASES), ((0, 8),), -0.2, 0.2)), 0.0009994507, 0.0099487305).astype(jnp.bfloat16),
        "species_opacity_factor": jnp.clip(jnp.exp(jax.random.uniform(seeds[2], (GASES,), jnp.float32, math.log(0.05), math.log(0.5))), 0.05, 0.5),
        "absorber_molefraction": jnp.clip(1.0 * jax.random.uniform(seeds[3], (NX, NY, NZ), jnp.float32) ** shard_levels(seeds[3], (NX, NY, NZ), ((0, 4),), -0.2, 0.2), 0.0, 1.0),
        "scaled_heat_level": draw_scaled_heat_level(jax.random.fold_in(seeds[7], 71), 0),
        "wall_touching_flag": place_ends((jax.random.randint(seeds[5], (NX, NY, NZ), 0, 4) < 1).astype(jnp.int32), jax.random.fold_in(seeds[5], 1), 0, 1),
        "fraction_polynomial": draw_fraction_polynomial(jax.random.fold_in(seeds[7], 71), 0),
    }


KAPPA_FLOOR = 0.5
WALL_LOSS = 0.5
LAM_LOW = 0.5
LAM_HIGH = 12.0


def neighbours(padded):
    return (padded[:, :-2, 1:-1, 1:-1], padded[:, 2:, 1:-1, 1:-1],
            padded[:, 1:-1, :-2, 1:-1], padded[:, 1:-1, 2:, 1:-1],
            padded[:, 1:-1, 1:-1, :-2], padded[:, 1:-1, 1:-1, 2:])


def widen(values):
    return jnp.pad(values, ((0, 0), (1, 1), (1, 1), (1, 1)))


def operate(values, diagonal, couple):
    beside = neighbours(widen(values))
    applied = diagonal * values
    for weight_face, neighbour in zip(couple, beside):
        applied = applied - weight_face * neighbour
    return applied


def reference(particle_amount, section_opacity, species_opacity_factor, absorber_molefraction, scaled_heat_level, wall_touching_flag, fraction_polynomial):
    soot_flat = particle_amount.reshape(particle_amount.shape[0], -1)
    soot_term = jnp.dot(section_opacity.T, soot_flat, preferred_element_type=jnp.float32)
    soot_term = soot_term.reshape((section_opacity.shape[1],) + absorber_molefraction.shape)
    absorption = KAPPA_FLOOR + species_opacity_factor[:, None, None, None] * absorber_molefraction[None] + soot_term
    heat_level_square = scaled_heat_level * scaled_heat_level
    component_fractions = fraction_polynomial[:, 0][:, None, None, None] + fraction_polynomial[:, 1][:, None, None, None] * scaled_heat_level[None] + fraction_polynomial[:, 2][:, None, None, None] * heat_level_square[None]
    emitted_power = component_fractions * (heat_level_square * heat_level_square)[None]
    couple = tuple(2.0 / (3.0 * (absorption + neighbour)) for neighbour in neighbours(widen(absorption)))
    diagonal = absorption + WALL_LOSS * wall_touching_flag.astype(jnp.float32)[None]
    for weight_face in couple:
        diagonal = diagonal + weight_face
    centre = (LAM_HIGH + LAM_LOW) / 2.0
    spread_half = (LAM_HIGH - LAM_LOW) / 2.0
    ratio_sigma = centre / spread_half
    residual = absorption * emitted_power
    direction = residual / centre
    iterate = jnp.zeros_like(residual)
    ratio_now = 1.0 / ratio_sigma
    for sweep_index in range(SWEEPS):
        iterate = iterate + direction
        residual = residual - operate(direction, diagonal, couple)
        ratio_next = 1.0 / (2.0 * ratio_sigma - ratio_now)
        direction = (ratio_next * ratio_now) * direction + (2.0 * ratio_next / spread_half) * residual
        ratio_now = ratio_next
    divergence = jnp.sum(absorption * (emitted_power - iterate), axis=0)
    average_radiative_loss = jnp.sum(divergence) / (NX * NY * NZ)
    return divergence, average_radiative_loss
```

```python
import functools

import jax
import jax.numpy as jnp
from jax import lax
from jax.experimental import pallas as pl
from jax.experimental.pallas import tpu as pltpu
from jax.sharding import PartitionSpec as P

SWEEPS = 6
HALO = SWEEPS - 1
KAPPA_FLOOR = 0.5
WALL_LOSS = 0.5
LAM_LOW = 0.5
LAM_HIGH = 12.0
CENTRE = (LAM_HIGH + LAM_LOW) / 2.0
SPREAD = (LAM_HIGH - LAM_LOW) / 2.0
MESH = pl.DeviceIdType.MESH


def reversed_bits(index, bits):
    return sum(((index >> b) & 1) << (bits - 1 - b) for b in range(bits))


def coupling(total):
    positive = total > 0.0
    return jnp.where(positive, 2.0 / (3.0 * jnp.where(positive, total, 1.0)), 0.0)


def kernel(
    n, spaces, slabs, cells,
    kron, amount, strength, mole, heat, flag, poly,
    out, average,
    amount_v, acc, recvs, absorb, heat_w, wall_w, cx, cy, cz, diag, res, rem, dirs,
    parts, totals, mine,
    load_sem, rs_send, rs_recv, halo_send, halo_recv, sum_send, sum_recv,
    gather_send, gather_recv, total_send, total_recv,
):
    bits = n.bit_length() - 1
    me, place = lax.axis_index("gas"), lax.axis_index("space")
    per_gas = acc.shape[2]
    x_rows, rows = heat.shape[0], heat_w.shape[0]
    slab_rows = x_rows // slabs
    order = [0, slabs - 1] + list(range(1, slabs - 1))

    def load(slab):
        return pltpu.make_async_copy(
            amount.at[:, pl.ds(slab * slab_rows, slab_rows)], amount_v.at[slab], load_sem.at[slab]
        )

    for slab in order:
        load(slab).start()

    barrier = pltpu.get_barrier_semaphore()
    for k in range(1, n):
        pl.semaphore_signal(
            barrier, inc=1, device_id={"gas": lax.rem(me + k, n)}, device_id_type=MESH
        )
    for k in range(1, spaces):
        pl.semaphore_signal(
            barrier, inc=1, device_id={"space": lax.rem(place + k, spaces)}, device_id_type=MESH
        )
    heat_w[HALO : HALO + x_rows] = heat[...]
    wall_w[HALO : HALO + x_rows] = WALL_LOSS * flag[...].astype(jnp.float32)
    pl.semaphore_wait(barrier, n - 1 + spaces - 1)

    right, left = lax.rem(place + 1, spaces), lax.rem(place + spaces - 1, spaces)

    def halo_pair(which, before, after, to_right, to_left):
        return [
            pltpu.make_async_remote_copy(
                src_ref=to_right, dst_ref=before,
                send_sem=halo_send.at[which, 0], recv_sem=halo_recv.at[which, 0],
                device_id={"space": right}, device_id_type=MESH,
            ),
            pltpu.make_async_remote_copy(
                src_ref=to_left, dst_ref=after,
                send_sem=halo_send.at[which, 1], recv_sem=halo_recv.at[which, 1],
                device_id={"space": left}, device_id_type=MESH,
            ),
        ]

    pairs = []
    for which, ref in enumerate((heat_w, wall_w)):
        pairs += halo_pair(
            which,
            ref.at[pl.ds(0, HALO)], ref.at[pl.ds(HALO + x_rows, HALO)],
            ref.at[pl.ds(x_rows, HALO)], ref.at[pl.ds(HALO, HALO)],
        )
    for copy in pairs:
        copy.start()

    bases, size = [jnp.int32(0)], n
    for stage in range(bits):
        size //= 2
        bases.append(bases[-1] + ((me >> stage) & 1) * size)
    position = bases[bits]

    def exchange(stage, slab):
        half = n >> (stage + 1)
        bit = (me >> stage) & 1
        partner = me + (1 - 2 * bit) * (1 << stage)
        return pltpu.make_async_remote_copy(
            src_ref=acc.at[slab, pl.ds(bases[stage] + (1 - bit) * half, half)],
            dst_ref=recvs[stage].at[slab],
            send_sem=rs_send.at[stage, slab], recv_sem=rs_recv.at[stage, slab],
            device_id={"gas": partner}, device_id_type=MESH,
        )

    def opacity(slab):
        load(slab).wait()

        def one(x, carry):
            block = amount_v[slab, :, x].reshape(-1, cells)
            value = jnp.dot(kron[...], block, preferred_element_type=jnp.float32)
            acc[slab, :, :, x] = value.reshape((n, per_gas) + acc.shape[4:])
            return carry

        lax.fori_loop(0, slab_rows, one, 0)

    absorb_pair = halo_pair(
        2,
        absorb.at[:, pl.ds(0, HALO)], absorb.at[:, pl.ds(HALO + x_rows, HALO)],
        absorb.at[:, pl.ds(x_rows, HALO)], absorb.at[:, pl.ds(HALO, HALO)],
    )

    for step in range(slabs + bits):
        if step < slabs:
            opacity(order[step])
            exchange(0, order[step]).start()
        for stage in range(bits):
            at = step - stage - 1
            if not 0 <= at < slabs:
                continue
            slab = order[at]
            exchange(stage, slab).wait_recv()
            if stage < bits - 1:
                half = n >> (stage + 1)
                kept = pl.ds(bases[stage + 1], half)
                acc[slab, kept] = acc[slab, kept] + recvs[stage][slab]
                exchange(stage + 1, slab).start()
            else:
                inner = pl.ds(slab * slab_rows, slab_rows)
                for i in range(per_gas):
                    absorb[i, pl.ds(HALO + slab * slab_rows, slab_rows)] = (
                        KAPPA_FLOOR + strength[me * per_gas + i] * mole[inner]
                        + (acc[slab, position, i] + recvs[stage][slab, 0, i])
                    )
                if at == 1:
                    for copy in absorb_pair:
                        copy.start()

    for copy in pairs + absorb_pair:
        copy.wait()
    absorb[:, 0:HALO] = jnp.where(place == 0, 0.0, absorb[:, 0:HALO])
    absorb[:, HALO + x_rows :] = jnp.where(place == spaces - 1, 0.0, absorb[:, HALO + x_rows :])

    tile = heat.shape[1:]
    y_at = lax.broadcasted_iota(jnp.int32, tile, 0)
    z_at = lax.broadcasted_iota(jnp.int32, tile, 1)
    y_low, y_top = y_at == 0, y_at == tile[0] - 1
    z_low, z_top = z_at == 0, z_at == tile[1] - 1

    def begin(i, row):
        level = heat_w[row]
        square = level * level
        gas = me * per_gas + i
        emitted = (poly[gas, 0] + poly[gas, 1] * level + poly[gas, 2] * square) * (square * square)
        first = absorb[i, row] * emitted
        rem[i, row] = emitted
        res[i, row] = first
        dirs[0, i, row] = first / CENTRE

    for i in range(per_gas):
        begin(i, 0)
        begin(i, rows - 1)

    def face(a, b):
        full = coupling(a + b)
        return full, jnp.where((a > 0.0) & (b > 0.0), full, 0.0)

    lowest = []
    for i in range(per_gas):
        full, off = face(absorb[i, 0], absorb[i, 1])
        cx[i, 1] = off
        lowest.append(full)

    def prepare(row, before):
        following = []
        for i in range(per_gas):
            begin(i, row)
            here = absorb[i, row]
            upper, off = face(here, absorb[i, row + 1])
            cx[i, row + 1] = off
            following.append(upper)
            edge = coupling(here)
            y_face = coupling(here + pltpu.roll(here, 1, 0))
            z_face = coupling(here + pltpu.roll(here, 1, 1))
            cy[i, row] = jnp.where(y_low, 0.0, y_face)
            cz[i, row] = jnp.where(z_low, 0.0, z_face)
            y_up = jnp.where(y_top, edge, pltpu.roll(y_face, tile[0] - 1, 0))
            z_up = jnp.where(z_top, edge, pltpu.roll(z_face, tile[1] - 1, 1))
            diag[i, row] = (
                here + wall_w[row] + before[i] + upper
                + jnp.where(y_low, edge, y_face) + y_up
                + jnp.where(z_low, edge, z_face) + z_up
            )
        return tuple(following)

    lax.fori_loop(1, rows - 1, prepare, tuple(lowest))

    sigma = CENTRE / SPREAD
    ratio = 1.0 / sigma
    for sweep in range(SWEEPS - 1):
        following = 1.0 / (2.0 * sigma - ratio)
        keep, gain = following * ratio, 2.0 * following / SPREAD
        ratio = following
        source, target = sweep % 2, (sweep + 1) % 2

        def relax(row, carry):
            for i in range(per_gas):
                d = dirs[source, i, row]
                c_y, c_z = cy[i, row], cz[i, row]
                applied = diag[i, row] * d
                applied -= cx[i, row] * dirs[source, i, row - 1]
                applied -= cx[i, row + 1] * dirs[source, i, row + 1]
                applied -= c_y * pltpu.roll(d, 1, 0) + pltpu.roll(c_y * d, tile[0] - 1, 0)
                applied -= c_z * pltpu.roll(d, 1, 1) + pltpu.roll(c_z * d, tile[1] - 1, 1)
                left_over = res[i, row] - applied
                res[i, row] = left_over
                rem[i, row] = rem[i, row] - d
                dirs[target, i, row] = keep * d + gain * left_over
            return carry

        lax.fori_loop(1 + sweep, rows - 1 - sweep, relax, 0)

    inner = pl.ds(HALO, x_rows)
    last = (SWEEPS - 1) % 2

    def finish(x, carry):
        row = x + HALO
        total = absorb[0, row] * (rem[0, row] - dirs[last, 0, row])
        for i in range(1, per_gas):
            total += absorb[i, row] * (rem[i, row] - dirs[last, i, row])
        mine[x] = total
        return carry

    lax.fori_loop(0, x_rows, finish, 0)

    chunk = x_rows // n
    own = pl.ds(me * chunk, chunk)
    sends = []
    for k in range(1, n):
        peer = lax.rem(me + k, n)
        sends.append(pltpu.make_async_remote_copy(
            src_ref=mine.at[pl.ds(peer * chunk, chunk)], dst_ref=parts.at[k],
            send_sem=sum_send.at[k], recv_sem=sum_recv.at[k],
            device_id={"gas": peer}, device_id_type=MESH,
        ))
    for copy in sends:
        copy.start()
    total = mine[own]
    for k in range(1, n):
        sends[k - 1].wait_recv()
        total = total + parts[k]
    out[own] = total

    def gather(k, origin):
        held = pl.ds(origin * chunk, chunk)
        return pltpu.make_async_remote_copy(
            src_ref=out.at[held], dst_ref=out.at[held],
            send_sem=gather_send.at[k], recv_sem=gather_recv.at[k],
            device_id={"gas": lax.rem(me + k, n)}, device_id_type=MESH,
        )

    for k in range(1, n):
        gather(k, me).start()
    for k in range(1, n):
        gather(k, lax.rem(me + n - k, n)).wait_recv()

    totals[place] = jnp.sum(out[...], axis=0)

    def share(k, origin):
        return pltpu.make_async_remote_copy(
            src_ref=totals.at[origin], dst_ref=totals.at[origin],
            send_sem=total_send.at[k], recv_sem=total_recv.at[k],
            device_id={"space": lax.rem(place + k, spaces)}, device_id_type=MESH,
        )

    for k in range(1, spaces):
        share(k, place).start()
    for k in range(1, spaces):
        share(k, lax.rem(place + spaces - k, spaces)).wait_recv()
    whole = jnp.sum(jnp.sum(totals[...], axis=0))
    average[0, 0] = whole * (1.0 / (x_rows * spaces * tile[0] * tile[1]))

    for stage in range(bits):
        for slab in range(slabs):
            exchange(stage, slab).wait_send()
    for k in range(1, n):
        sends[k - 1].wait_send()
        gather(k, me).wait_send()
    for k in range(1, spaces):
        share(k, place).wait_send()


def per_device(
    n, spaces, particle_amount, section_opacity, species_opacity_factor,
    absorber_molefraction, scaled_heat_level, wall_touching_flag, fraction_polynomial,
):
    sections, x_rows, ny, nz = particle_amount.shape
    gases = section_opacity.shape[1]
    per_gas = gases // n
    bits = n.bit_length() - 1
    slabs = x_rows // 8
    owners = [reversed_bits(p, bits) for p in range(n)]
    by_place = jnp.concatenate(
        [section_opacity[:, o * per_gas : (o + 1) * per_gas] for o in owners], axis=1
    ).T
    kron = (by_place[:, None, :, None] * jnp.eye(ny, dtype=jnp.bfloat16)[None, :, None, :]).reshape(
        gases * ny, sections * ny
    )
    rows = x_rows + 2 * HALO
    slab_rows = x_rows // slabs
    field = pltpu.VMEM((per_gas, rows, ny, nz), jnp.float32)
    dma = pltpu.SemaphoreType.DMA
    vmem, smem = pl.BlockSpec(memory_space=pltpu.VMEM), pl.BlockSpec(memory_space=pltpu.SMEM)
    divergence, average = pl.pallas_call(
        functools.partial(kernel, n, spaces, slabs, nz),
        out_shape=(
            jax.ShapeDtypeStruct((x_rows, ny, nz), jnp.float32),
            jax.ShapeDtypeStruct((1, 1), jnp.float32),
        ),
        in_specs=[vmem, pl.BlockSpec(memory_space=pl.ANY), smem, vmem, vmem, vmem, smem],
        out_specs=(vmem, smem),
        scratch_shapes=[
            pltpu.VMEM((slabs, sections, slab_rows, ny, nz), jnp.bfloat16),
            pltpu.VMEM((slabs, n, per_gas, slab_rows, ny, nz), jnp.float32),
            [
                pltpu.VMEM((slabs, n >> (stage + 1), per_gas, slab_rows, ny, nz), jnp.float32)
                for stage in range(bits)
            ],
            field,
            pltpu.VMEM((rows, ny, nz), jnp.float32),
            pltpu.VMEM((rows, ny, nz), jnp.float32),
            field, field, field, field, field, field,
            pltpu.VMEM((2, per_gas, rows, ny, nz), jnp.float32),
            pltpu.VMEM((n, x_rows // n, ny, nz), jnp.float32),
            pltpu.VMEM((spaces, ny, nz), jnp.float32),
            pltpu.VMEM((x_rows, ny, nz), jnp.float32),
            dma((slabs,)), dma((bits, slabs)), dma((bits, slabs)), dma((3, 2)), dma((3, 2)),
            dma((n,)), dma((n,)), dma((n,)), dma((n,)), dma((spaces,)), dma((spaces,)),
        ],
        compiler_params=pltpu.CompilerParams(
            collective_id=0, has_side_effects=True, vmem_limit_bytes=56 * 1024 * 1024
        ),
    )(
        kron, particle_amount, species_opacity_factor, absorber_molefraction,
        scaled_heat_level, wall_touching_flag, fraction_polynomial,
    )
    return divergence, average.reshape(())


def solution(mesh):
    return jax.shard_map(
        functools.partial(per_device, mesh.shape["gas"], mesh.shape["space"]),
        mesh=mesh,
        in_specs=(
            P("gas", "space", None, None),
            P("gas", None),
            P(),
            P("space", None, None),
            P("space", None, None),
            P("space", None, None),
            P(),
        ),
        out_specs=(P("space", None, None), P()),
        check_vma=False,
    )
```

```python
import functools

import jax
import jax.numpy as jnp
from jax import lax
from jax.experimental import pallas as pl
from jax.experimental.pallas import tpu as pltpu
from jax.sharding import PartitionSpec as P

SWEEPS = 6
HALO = SWEEPS - 1
BLOCK = 4
KAPPA_FLOOR = 0.5
WALL_LOSS = 0.5
LAM_LOW = 0.5
LAM_HIGH = 12.0
CENTRE = (LAM_HIGH + LAM_LOW) / 2.0
SPREAD = (LAM_HIGH - LAM_LOW) / 2.0
MESH = pl.DeviceIdType.MESH


def reversed_bits(index, bits):
    return sum(((index >> b) & 1) << (bits - 1 - b) for b in range(bits))


def coupling(total):
    positive = total > 0.0
    return jnp.where(positive, 2.0 / (3.0 * jnp.where(positive, total, 1.0)), 0.0)


def kernel(
    n, spaces, slabs, cells,
    opacity_t, amount, strength, mole, heat, flag, poly,
    out, average,
    amount_v, acc, recvs, absorb, heat_w, wall_w, cx, cy, cz, diag, res, rem, dirs,
    parts, totals, mine, kron,
    load_sem, rs_send, rs_recv, halo_send, halo_recv, sum_send, sum_recv,
    gather_send, gather_recv, total_send, total_recv,
):
    bits = n.bit_length() - 1
    me, place = lax.axis_index("gas"), lax.axis_index("space")
    per_gas = acc.shape[2]
    x_rows, rows = heat.shape[0], heat_w.shape[0]
    slab_rows = x_rows // slabs
    order = [0, slabs - 1] + list(range(1, slabs - 1))

    def load(slab):
        return pltpu.make_async_copy(
            amount.at[:, pl.ds(slab * slab_rows, slab_rows)], amount_v.at[slab], load_sem.at[slab]
        )

    for slab in order:
        load(slab).start()

    barrier = pltpu.get_barrier_semaphore()
    for k in range(1, n):
        pl.semaphore_signal(
            barrier, inc=1, device_id={"gas": lax.rem(me + k, n)}, device_id_type=MESH
        )
    for k in range(1, spaces):
        pl.semaphore_signal(
            barrier, inc=1, device_id={"space": lax.rem(place + k, spaces)}, device_id_type=MESH
        )
    heat_w[HALO : HALO + x_rows] = heat[...]
    wall_w[HALO : HALO + x_rows] = WALL_LOSS * flag[...].astype(jnp.float32)
    gases, sections = opacity_t.shape
    ny = heat.shape[1]
    line = lax.broadcasted_iota(jnp.int32, (gases * ny, gases), 0) // ny
    wanted = reversed_bits(line // per_gas, bits) * per_gas + line % per_gas
    picks = wanted == lax.broadcasted_iota(jnp.int32, (gases * ny, gases), 1)
    spread = lax.broadcasted_iota(jnp.int32, (sections, sections * ny), 1) // ny
    widens = spread == lax.broadcasted_iota(jnp.int32, (sections, sections * ny), 0)
    rows_of = jnp.dot(
        jnp.where(picks, 1.0, 0.0).astype(jnp.bfloat16), opacity_t[...],
        preferred_element_type=jnp.float32,
    ).astype(jnp.bfloat16)
    wide = jnp.dot(
        rows_of, jnp.where(widens, 1.0, 0.0).astype(jnp.bfloat16),
        preferred_element_type=jnp.float32,
    )
    same = (
        lax.broadcasted_iota(jnp.int32, wide.shape, 0) % ny
        == lax.broadcasted_iota(jnp.int32, wide.shape, 1) % ny
    )
    kron[...] = jnp.where(same, wide, 0.0).astype(jnp.bfloat16)
    pl.semaphore_wait(barrier, n - 1 + spaces - 1)

    right, left = lax.rem(place + 1, spaces), lax.rem(place + spaces - 1, spaces)

    def halo_pair(which, before, after, to_right, to_left):
        return [
            pltpu.make_async_remote_copy(
                src_ref=to_right, dst_ref=before,
                send_sem=halo_send.at[which, 0], recv_sem=halo_recv.at[which, 0],
                device_id={"space": right}, device_id_type=MESH,
            ),
            pltpu.make_async_remote_copy(
                src_ref=to_left, dst_ref=after,
                send_sem=halo_send.at[which, 1], recv_sem=halo_recv.at[which, 1],
                device_id={"space": left}, device_id_type=MESH,
            ),
        ]

    pairs = []
    for which, ref in enumerate((heat_w, wall_w)):
        pairs += halo_pair(
            which,
            ref.at[pl.ds(0, HALO)], ref.at[pl.ds(HALO + x_rows, HALO)],
            ref.at[pl.ds(x_rows, HALO)], ref.at[pl.ds(HALO, HALO)],
        )
    for copy in pairs:
        copy.start()

    bases, size = [jnp.int32(0)], n
    for stage in range(bits):
        size //= 2
        bases.append(bases[-1] + ((me >> stage) & 1) * size)
    position = bases[bits]

    def exchange(stage, slab):
        half = n >> (stage + 1)
        bit = (me >> stage) & 1
        partner = me + (1 - 2 * bit) * (1 << stage)
        return pltpu.make_async_remote_copy(
            src_ref=acc.at[slab, pl.ds(bases[stage] + (1 - bit) * half, half)],
            dst_ref=recvs[stage].at[slab],
            send_sem=rs_send.at[stage, slab], recv_sem=rs_recv.at[stage, slab],
            device_id={"gas": partner}, device_id_type=MESH,
        )

    def opacity(slab):
        load(slab).wait()

        def one(x, carry):
            column = amount_v[slab, :, x].reshape(-1, cells)
            value = jnp.dot(kron[...], column, preferred_element_type=jnp.float32)
            acc[slab, :, :, x] = value.reshape((n, per_gas) + acc.shape[4:])
            return carry

        lax.fori_loop(0, slab_rows, one, 0)

    absorb_pair = halo_pair(
        2,
        absorb.at[:, pl.ds(0, HALO)], absorb.at[:, pl.ds(HALO + x_rows, HALO)],
        absorb.at[:, pl.ds(x_rows, HALO)], absorb.at[:, pl.ds(HALO, HALO)],
    )

    for step in range(slabs + bits):
        if step < slabs:
            opacity(order[step])
            exchange(0, order[step]).start()
        for stage in range(bits):
            at = step - stage - 1
            if not 0 <= at < slabs:
                continue
            slab = order[at]
            exchange(stage, slab).wait_recv()
            if stage < bits - 1:
                half = n >> (stage + 1)
                kept = pl.ds(bases[stage + 1], half)
                acc[slab, kept] = acc[slab, kept] + recvs[stage][slab]
                exchange(stage + 1, slab).start()
            else:
                inner = pl.ds(slab * slab_rows, slab_rows)
                for i in range(per_gas):
                    absorb[i, pl.ds(HALO + slab * slab_rows, slab_rows)] = (
                        KAPPA_FLOOR + strength[me * per_gas + i] * mole[inner]
                        + (acc[slab, position, i] + recvs[stage][slab, 0, i])
                    )
                if at == 1:
                    for copy in absorb_pair:
                        copy.start()

    for copy in pairs + absorb_pair:
        copy.wait()
    absorb[:, 0:HALO] = jnp.where(place == 0, 0.0, absorb[:, 0:HALO])
    absorb[:, HALO + x_rows :] = jnp.where(place == spaces - 1, 0.0, absorb[:, HALO + x_rows :])

    tile = heat.shape[1:]
    block = (BLOCK,) + tile
    y_at = lax.broadcasted_iota(jnp.int32, block, 1)
    z_at = lax.broadcasted_iota(jnp.int32, block, 2)
    y_low, y_top = y_at == 0, y_at == tile[0] - 1
    z_low, z_top = z_at == 0, z_at == tile[1] - 1

    def begin(i, at):
        level = heat_w[at]
        square = level * level
        gas = me * per_gas + i
        emitted = (poly[0, gas] + poly[1, gas] * level + poly[2, gas] * square) * (square * square)
        first = absorb[i, at] * emitted
        return emitted, first, first / CENTRE

    def put_begin(i, at, values):
        rem[i, at], res[i, at], dirs[0, i, at] = values

    def face(a, b):
        full = coupling(a + b)
        return full, jnp.where((a > 0.0) & (b > 0.0), full, 0.0)

    for i in range(per_gas):
        for at in (pl.ds(0, 1), pl.ds(rows - 1, 1)):
            put_begin(i, at, begin(i, at))
            dirs[1, i, at] = jnp.zeros((1,) + tile, jnp.float32)
        cx[i, rows - 1] = face(absorb[i, rows - 2], absorb[i, rows - 1])[1]

    def prepare(step, carry):
        row = 1 + step * BLOCK
        at = pl.ds(row, BLOCK)
        found = []
        for i in range(per_gas):
            around = absorb[i, pl.ds(row - 1, BLOCK + 2)]
            here = around[1:-1]
            full, off = face(around[:-1], around[1:])
            edge = coupling(here)
            y_face = coupling(here + pltpu.roll(here, 1, 1))
            z_face = coupling(here + pltpu.roll(here, 1, 2))
            y_up = jnp.where(y_top, edge, pltpu.roll(y_face, tile[0] - 1, 1))
            z_up = jnp.where(z_top, edge, pltpu.roll(z_face, tile[1] - 1, 2))
            middle = (
                here + wall_w[at] + full[:-1] + full[1:]
                + jnp.where(y_low, edge, y_face) + y_up
                + jnp.where(z_low, edge, z_face) + z_up
            )
            found.append((
                off[:-1], jnp.where(y_low, 0.0, y_face), jnp.where(z_low, 0.0, z_face), middle,
                begin(i, at),
            ))
        for i in range(per_gas):
            cx[i, at], cy[i, at], cz[i, at], diag[i, at], values = found[i]
            put_begin(i, at, values)
        return carry

    lax.fori_loop(0, (rows - 2) // BLOCK, prepare, 0)

    sigma = CENTRE / SPREAD
    ratio = 1.0 / sigma
    for sweep in range(SWEEPS - 1):
        following = 1.0 / (2.0 * sigma - ratio)
        keep, gain = following * ratio, 2.0 * following / SPREAD
        ratio = following
        source, target = sweep % 2, (sweep + 1) % 2
        skip = sweep * 2 // BLOCK * BLOCK // 2

        def relax(step, carry):
            row = 1 + skip + step * BLOCK
            at = pl.ds(row, BLOCK)
            found = []
            for i in range(per_gas):
                around = dirs[source, i, pl.ds(row - 1, BLOCK + 2)]
                d = around[1:-1]
                c_x, c_y, c_z = cx[i, pl.ds(row, BLOCK + 1)], cy[i, at], cz[i, at]
                applied = diag[i, at] * d
                applied -= c_x[:-1] * around[:-2]
                applied -= c_x[1:] * around[2:]
                applied -= c_y * pltpu.roll(d, 1, 1) + pltpu.roll(c_y * d, tile[0] - 1, 1)
                applied -= c_z * pltpu.roll(d, 1, 2) + pltpu.roll(c_z * d, tile[1] - 1, 2)
                left_over = res[i, at] - applied
                found.append((left_over, rem[i, at] - d, keep * d + gain * left_over))
            for i in range(per_gas):
                res[i, at], rem[i, at], dirs[target, i, at] = found[i]
            return carry

        lax.fori_loop(0, (rows - 2 - 2 * skip) // BLOCK, relax, 0)

    last = (SWEEPS - 1) % 2

    def finish(step, carry):
        at = pl.ds(HALO + step * BLOCK, BLOCK)
        total = absorb[0, at] * (rem[0, at] - dirs[last, 0, at])
        for i in range(1, per_gas):
            total += absorb[i, at] * (rem[i, at] - dirs[last, i, at])
        mine[pl.ds(step * BLOCK, BLOCK)] = total
        return carry

    lax.fori_loop(0, x_rows // BLOCK, finish, 0)

    chunk = x_rows // n
    own = pl.ds(me * chunk, chunk)
    sends = []
    for k in range(1, n):
        peer = lax.rem(me + k, n)
        sends.append(pltpu.make_async_remote_copy(
            src_ref=mine.at[pl.ds(peer * chunk, chunk)], dst_ref=parts.at[k],
            send_sem=sum_send.at[k], recv_sem=sum_recv.at[k],
            device_id={"gas": peer}, device_id_type=MESH,
        ))
    for copy in sends:
        copy.start()
    total = mine[own]
    for k in range(1, n):
        sends[k - 1].wait_recv()
        total = total + parts[k]
    out[own] = total

    def gather(k, origin):
        held = pl.ds(origin * chunk, chunk)
        return pltpu.make_async_remote_copy(
            src_ref=out.at[held], dst_ref=out.at[held],
            send_sem=gather_send.at[k], recv_sem=gather_recv.at[k],
            device_id={"gas": lax.rem(me + k, n)}, device_id_type=MESH,
        )

    for k in range(1, n):
        gather(k, me).start()
    for k in range(1, n):
        gather(k, lax.rem(me + n - k, n)).wait_recv()

    totals[place] = jnp.sum(out[...], axis=0)

    def share(k, origin):
        return pltpu.make_async_remote_copy(
            src_ref=totals.at[origin], dst_ref=totals.at[origin],
            send_sem=total_send.at[k], recv_sem=total_recv.at[k],
            device_id={"space": lax.rem(place + k, spaces)}, device_id_type=MESH,
        )

    for k in range(1, spaces):
        share(k, place).start()
    for k in range(1, spaces):
        share(k, lax.rem(place + spaces - k, spaces)).wait_recv()
    whole = jnp.sum(jnp.sum(totals[...], axis=0))
    average[0, 0] = whole * (1.0 / (x_rows * spaces * tile[0] * tile[1]))

    for stage in range(bits):
        for slab in range(slabs):
            exchange(stage, slab).wait_send()
    for k in range(1, n):
        sends[k - 1].wait_send()
        gather(k, me).wait_send()
    for k in range(1, spaces):
        share(k, place).wait_send()


def per_device(
    n, spaces, particle_amount, section_opacity, species_opacity_factor,
    absorber_molefraction, scaled_heat_level, wall_touching_flag, fraction_polynomial,
):
    sections, x_rows, ny, nz = particle_amount.shape
    gases = section_opacity.shape[1]
    per_gas = gases // n
    bits = n.bit_length() - 1
    slabs = x_rows // 8
    rows = x_rows + 2 * HALO
    slab_rows = x_rows // slabs
    field = pltpu.VMEM((per_gas, rows, ny, nz), jnp.float32)
    dma = pltpu.SemaphoreType.DMA
    vmem, smem = pl.BlockSpec(memory_space=pltpu.VMEM), pl.BlockSpec(memory_space=pltpu.SMEM)
    divergence, average = pl.pallas_call(
        functools.partial(kernel, n, spaces, slabs, nz),
        out_shape=(
            jax.ShapeDtypeStruct((x_rows, ny, nz), jnp.float32),
            jax.ShapeDtypeStruct((1, 1), jnp.float32),
        ),
        in_specs=[vmem, pl.BlockSpec(memory_space=pl.ANY), smem, vmem, vmem, vmem, smem],
        out_specs=(vmem, smem),
        scratch_shapes=[
            pltpu.VMEM((slabs, sections, slab_rows, ny, nz), jnp.bfloat16),
            pltpu.VMEM((slabs, n, per_gas, slab_rows, ny, nz), jnp.float32),
            [
                pltpu.VMEM((slabs, n >> (stage + 1), per_gas, slab_rows, ny, nz), jnp.float32)
                for stage in range(bits)
            ],
            field,
            pltpu.VMEM((rows, ny, nz), jnp.float32),
            pltpu.VMEM((rows, ny, nz), jnp.float32),
            field, field, field, field, field, field,
            pltpu.VMEM((2, per_gas, rows, ny, nz), jnp.float32),
            pltpu.VMEM((n, x_rows // n, ny, nz), jnp.float32),
            pltpu.VMEM((spaces, ny, nz), jnp.float32),
            pltpu.VMEM((x_rows, ny, nz), jnp.float32),
            pltpu.VMEM((gases * ny, sections * ny), jnp.bfloat16),
            dma((slabs,)), dma((bits, slabs)), dma((bits, slabs)), dma((3, 2)), dma((3, 2)),
            dma((n,)), dma((n,)), dma((n,)), dma((n,)), dma((spaces,)), dma((spaces,)),
        ],
        compiler_params=pltpu.CompilerParams(
            collective_id=0, has_side_effects=True, vmem_limit_bytes=56 * 1024 * 1024
        ),
    )(
        section_opacity.T, particle_amount, species_opacity_factor, absorber_molefraction,
        scaled_heat_level, wall_touching_flag, fraction_polynomial.T,
    )
    return divergence, average.reshape(())


def solution(mesh):
    return jax.shard_map(
        functools.partial(per_device, mesh.shape["gas"], mesh.shape["space"]),
        mesh=mesh,
        in_specs=(
            P("gas", "space", None, None),
            P("gas", None),
            P(),
            P("space", None, None),
            P("space", None, None),
            P("space", None, None),
            P(),
        ),
        out_specs=(P("space", None, None), P()),
        check_vma=False,
    )
```

```python
import functools

import jax
import jax.numpy as jnp
from jax import lax
from jax.experimental import pallas as pl
from jax.experimental.pallas import tpu as pltpu
from jax.sharding import PartitionSpec as P

SWEEPS = 6
HALO = SWEEPS - 1
BLOCK = 4
AHEAD = 3
SLAB_ROWS = 8
Z_FIRST = (1,)
KAPPA_FLOOR = 0.5
WALL_LOSS = 0.5
LAM_LOW = 0.5
LAM_HIGH = 12.0
CENTRE = (LAM_HIGH + LAM_LOW) / 2.0
SPREAD = (LAM_HIGH - LAM_LOW) / 2.0
MESH = pl.DeviceIdType.MESH


def coupling(total):
    positive = total > 0.0
    return jnp.where(positive, 2.0 / (3.0 * jnp.where(positive, total, 1.0)), 0.0)


def kernel(
    n, spaces, slabs, cells,
    opacity_t, amount, strength, mole, heat, flag, poly,
    out, average,
    amount_v, acc, recvs, absorb, heat_w, wall_w, cx, cy, cz, diag, res, rem, dirs,
    parts, totals, gas_totals, mine, kron,
    load_sem, rs_send, rs_recv, halo_send, halo_recv, sum_send, sum_recv,
    gather_send, gather_recv, total_send, total_recv, greet_send, greet_recv,
):
    bits = n.bit_length() - 1
    me, place = lax.axis_index("gas"), lax.axis_index("space")
    per_gas = acc.shape[2]
    x_rows, rows = heat.shape[0], heat_w.shape[0]
    slab_rows = x_rows // slabs
    edge = -(-HALO // slab_rows)
    order = (
        list(range(edge)) + list(range(slabs - edge, slabs)) + list(range(edge, slabs - edge))
    )
    low_first = list(range(bits))
    high_first = low_first[1:] + low_first[:1]
    bit_order = {
        slab: high_first if at % 8 in Z_FIRST else low_first for at, slab in enumerate(order)
    }

    def load(slab):
        return pltpu.make_async_copy(
            amount.at[:, pl.ds(slab * slab_rows, slab_rows)], amount_v.at[slab], load_sem.at[slab]
        )

    for slab in order[:AHEAD]:
        load(slab).start()

    barrier = pltpu.get_barrier_semaphore()
    for k in range(1, n):
        pl.semaphore_signal(
            barrier, inc=1, device_id={"gas": lax.rem(me + k, n)}, device_id_type=MESH
        )
    for k in range(1, spaces):
        pl.semaphore_signal(
            barrier, inc=1, device_id={"space": lax.rem(place + k, spaces)}, device_id_type=MESH
        )
    heat_w[HALO : HALO + x_rows] = heat[...]
    wall_w[HALO : HALO + x_rows] = WALL_LOSS * flag[...].astype(jnp.float32)
    gases, sections = opacity_t.shape
    ny = heat.shape[1]
    line = lax.broadcasted_iota(jnp.int32, (gases * ny, gases), 0) // ny
    picks = line == lax.broadcasted_iota(jnp.int32, (gases * ny, gases), 1)
    spread = lax.broadcasted_iota(jnp.int32, (sections, sections * ny), 1) // ny
    widens = spread == lax.broadcasted_iota(jnp.int32, (sections, sections * ny), 0)
    rows_of = jnp.dot(
        jnp.where(picks, 1.0, 0.0).astype(jnp.bfloat16), opacity_t[...],
        preferred_element_type=jnp.float32,
    ).astype(jnp.bfloat16)
    wide = jnp.dot(
        rows_of, jnp.where(widens, 1.0, 0.0).astype(jnp.bfloat16),
        preferred_element_type=jnp.float32,
    )
    same = (
        lax.broadcasted_iota(jnp.int32, wide.shape, 0) % ny
        == lax.broadcasted_iota(jnp.int32, wide.shape, 1) % ny
    )
    kron[...] = jnp.where(same, wide, 0.0).astype(jnp.bfloat16)
    pl.semaphore_wait(barrier, n - 1 + spaces - 1)

    right, left = lax.rem(place + 1, spaces), lax.rem(place + spaces - 1, spaces)

    def halo_pair(which, before, after, to_right, to_left):
        return [
            pltpu.make_async_remote_copy(
                src_ref=to_right, dst_ref=before,
                send_sem=halo_send.at[which, 0], recv_sem=halo_recv.at[which, 0],
                device_id={"space": right}, device_id_type=MESH,
            ),
            pltpu.make_async_remote_copy(
                src_ref=to_left, dst_ref=after,
                send_sem=halo_send.at[which, 1], recv_sem=halo_recv.at[which, 1],
                device_id={"space": left}, device_id_type=MESH,
            ),
        ]

    pairs = []
    for which, ref in enumerate((heat_w, wall_w)):
        pairs += halo_pair(
            which,
            ref.at[pl.ds(0, HALO)], ref.at[pl.ds(HALO + x_rows, HALO)],
            ref.at[pl.ds(x_rows, HALO)], ref.at[pl.ds(HALO, HALO)],
        )
    for copy in pairs:
        copy.start()

    def base(stage, slab):
        return sum(
            ((me >> bit) & 1) * (n >> (at + 1)) for at, bit in enumerate(bit_order[slab][:stage])
        ) + jnp.int32(0)

    def spot(owner, slab):
        return sum(
            ((owner >> bit) & 1) * (n >> (at + 1)) for at, bit in enumerate(bit_order[slab])
        )

    def exchange(stage, slab):
        half = n >> (stage + 1)
        level = bit_order[slab][stage]
        bit = (me >> level) & 1
        partner = me + (1 - 2 * bit) * (1 << level)
        return pltpu.make_async_remote_copy(
            src_ref=acc.at[slab, pl.ds(base(stage, slab) + (1 - bit) * half, half)],
            dst_ref=recvs[stage].at[slab],
            send_sem=rs_send.at[stage, slab], recv_sem=rs_recv.at[stage, slab],
            device_id={"gas": partner}, device_id_type=MESH,
        )

    def opacity(slab):
        load(slab).wait()

        def one(x, carry):
            column = amount_v[slab, :, x].reshape(-1, cells)
            value = jnp.dot(kron[...], column, preferred_element_type=jnp.float32)
            value = value.reshape((n, per_gas) + acc.shape[4:])
            for owner in range(n):
                acc[slab, spot(owner, slab), :, x] = value[owner]
            return carry

        lax.fori_loop(0, slab_rows, one, 0)

    absorb_pair = halo_pair(
        2,
        absorb.at[:, pl.ds(0, HALO)], absorb.at[:, pl.ds(HALO + x_rows, HALO)],
        absorb.at[:, pl.ds(x_rows, HALO)], absorb.at[:, pl.ds(HALO, HALO)],
    )

    for step in range(slabs + bits):
        if step < slabs:
            if step + AHEAD < slabs:
                load(order[step + AHEAD]).start()
            opacity(order[step])
            exchange(0, order[step]).start()
        for stage in range(bits):
            at = step - stage - 1
            if not 0 <= at < slabs:
                continue
            slab = order[at]
            exchange(stage, slab).wait_recv()
            if stage < bits - 1:
                half = n >> (stage + 1)
                kept = pl.ds(base(stage + 1, slab), half)
                acc[slab, kept] = acc[slab, kept] + recvs[stage][slab]
                exchange(stage + 1, slab).start()
            else:
                inner = pl.ds(slab * slab_rows, slab_rows)
                for i in range(per_gas):
                    absorb[i, pl.ds(HALO + slab * slab_rows, slab_rows)] = (
                        KAPPA_FLOOR + strength[me * per_gas + i] * mole[inner]
                        + (acc[slab, base(bits, slab), i] + recvs[stage][slab, 0, i])
                    )
                if at == 2 * edge - 1:
                    for copy in absorb_pair:
                        copy.start()

    for copy in pairs + absorb_pair:
        copy.wait()
    absorb[:, 0:HALO] = jnp.where(place == 0, 0.0, absorb[:, 0:HALO])
    absorb[:, HALO + x_rows :] = jnp.where(place == spaces - 1, 0.0, absorb[:, HALO + x_rows :])

    tile = heat.shape[1:]
    block = (BLOCK,) + tile
    y_at = lax.broadcasted_iota(jnp.int32, block, 1)
    z_at = lax.broadcasted_iota(jnp.int32, block, 2)
    y_low, y_top = y_at == 0, y_at == tile[0] - 1
    z_low, z_top = z_at == 0, z_at == tile[1] - 1

    def begin(i, at):
        level = heat_w[at]
        square = level * level
        gas = me * per_gas + i
        emitted = (poly[0, gas] + poly[1, gas] * level + poly[2, gas] * square) * (square * square)
        first = absorb[i, at] * emitted
        return emitted, first, first / CENTRE

    def put_begin(i, at, values):
        rem[i, at], res[i, at], dirs[0, i, at] = values

    def face(a, b):
        full = coupling(a + b)
        return full, jnp.where((a > 0.0) & (b > 0.0), full, 0.0)

    for i in range(per_gas):
        for at in (pl.ds(0, 1), pl.ds(rows - 1, 1)):
            put_begin(i, at, begin(i, at))
            dirs[1, i, at] = jnp.zeros((1,) + tile, jnp.float32)
        cx[i, rows - 1] = face(absorb[i, rows - 2], absorb[i, rows - 1])[1]

    def prepare(step, carry):
        row = 1 + step * BLOCK
        at = pl.ds(row, BLOCK)
        found = []
        for i in range(per_gas):
            around = absorb[i, pl.ds(row - 1, BLOCK + 2)]
            here = around[1:-1]
            full, off = face(around[:-1], around[1:])
            edge = coupling(here)
            y_face = coupling(here + pltpu.roll(here, 1, 1))
            z_face = coupling(here + pltpu.roll(here, 1, 2))
            y_up = jnp.where(y_top, edge, pltpu.roll(y_face, tile[0] - 1, 1))
            z_up = jnp.where(z_top, edge, pltpu.roll(z_face, tile[1] - 1, 2))
            middle = (
                here + wall_w[at] + full[:-1] + full[1:]
                + jnp.where(y_low, edge, y_face) + y_up
                + jnp.where(z_low, edge, z_face) + z_up
            )
            found.append((
                off[:-1], jnp.where(y_low, 0.0, y_face), jnp.where(z_low, 0.0, z_face), middle,
                begin(i, at),
            ))
        for i in range(per_gas):
            cx[i, at], cy[i, at], cz[i, at], diag[i, at], values = found[i]
            put_begin(i, at, values)
        return carry

    lax.fori_loop(0, (rows - 2) // BLOCK, prepare, 0)

    sigma = CENTRE / SPREAD
    ratio = 1.0 / sigma
    for sweep in range(SWEEPS - 1):
        following = 1.0 / (2.0 * sigma - ratio)
        keep, gain = following * ratio, 2.0 * following / SPREAD
        ratio = following
        source, target = sweep % 2, (sweep + 1) % 2
        skip = sweep * 2 // BLOCK * BLOCK // 2

        def relax(step, carry):
            row = 1 + skip + step * BLOCK
            at = pl.ds(row, BLOCK)
            found = []
            for i in range(per_gas):
                around = dirs[source, i, pl.ds(row - 1, BLOCK + 2)]
                d = around[1:-1]
                c_x, c_y, c_z = cx[i, pl.ds(row, BLOCK + 1)], cy[i, at], cz[i, at]
                applied = diag[i, at] * d
                applied -= c_x[:-1] * around[:-2]
                applied -= c_x[1:] * around[2:]
                applied -= c_y * pltpu.roll(d, 1, 1) + pltpu.roll(c_y * d, tile[0] - 1, 1)
                applied -= c_z * pltpu.roll(d, 1, 2) + pltpu.roll(c_z * d, tile[1] - 1, 2)
                left_over = res[i, at] - applied
                found.append((left_over, rem[i, at] - d, keep * d + gain * left_over))
            for i in range(per_gas):
                res[i, at], rem[i, at], dirs[target, i, at] = found[i]
            return carry

        lax.fori_loop(0, (rows - 2 - 2 * skip) // BLOCK, relax, 0)

    last = (SWEEPS - 1) % 2

    def finish(step, carry):
        at = pl.ds(HALO + step * BLOCK, BLOCK)
        total = absorb[0, at] * (rem[0, at] - dirs[last, 0, at])
        for i in range(1, per_gas):
            total += absorb[i, at] * (rem[i, at] - dirs[last, i, at])
        mine[pl.ds(step * BLOCK, BLOCK)] = total
        return carry + jnp.sum(total, axis=0)

    gas_totals[me] = lax.fori_loop(
        0, x_rows // BLOCK, finish, jnp.zeros(tile, jnp.float32)
    )

    chunk = x_rows // n
    own = pl.ds(me * chunk, chunk)
    sends = []
    for k in range(1, n):
        peer = lax.rem(me + k, n)
        sends.append(pltpu.make_async_remote_copy(
            src_ref=mine.at[pl.ds(peer * chunk, chunk)], dst_ref=parts.at[k],
            send_sem=sum_send.at[k], recv_sem=sum_recv.at[k],
            device_id={"gas": peer}, device_id_type=MESH,
        ))
    def greet(k, origin):
        return pltpu.make_async_remote_copy(
            src_ref=gas_totals.at[origin], dst_ref=gas_totals.at[origin],
            send_sem=greet_send.at[k], recv_sem=greet_recv.at[k],
            device_id={"gas": lax.rem(me + k, n)}, device_id_type=MESH,
        )

    for k in range(1, n):
        greet(k, me).start()
    for copy in sends:
        copy.start()
    total = mine[own]
    for k in range(1, n):
        sends[k - 1].wait_recv()
        total = total + parts[k]
    out[own] = total

    def gather(k, origin):
        held = pl.ds(origin * chunk, chunk)
        return pltpu.make_async_remote_copy(
            src_ref=out.at[held], dst_ref=out.at[held],
            send_sem=gather_send.at[k], recv_sem=gather_recv.at[k],
            device_id={"gas": lax.rem(me + k, n)}, device_id_type=MESH,
        )

    for k in range(1, n):
        gather(k, me).start()
    for k in range(1, n):
        greet(k, lax.rem(me + n - k, n)).wait_recv()
    totals[place] = jnp.sum(gas_totals[...], axis=0)

    def share(k, origin):
        return pltpu.make_async_remote_copy(
            src_ref=totals.at[origin], dst_ref=totals.at[origin],
            send_sem=total_send.at[k], recv_sem=total_recv.at[k],
            device_id={"space": lax.rem(place + k, spaces)}, device_id_type=MESH,
        )

    for k in range(1, spaces):
        share(k, place).start()
    for k in range(1, spaces):
        share(k, lax.rem(place + spaces - k, spaces)).wait_recv()
    for k in range(1, n):
        gather(k, lax.rem(me + n - k, n)).wait_recv()
    whole = jnp.sum(jnp.sum(totals[...], axis=0))
    average[0, 0] = whole * (1.0 / (x_rows * spaces * tile[0] * tile[1]))

    for stage in range(bits):
        for slab in range(slabs):
            exchange(stage, slab).wait_send()
    for k in range(1, n):
        sends[k - 1].wait_send()
        gather(k, me).wait_send()
        greet(k, me).wait_send()
    for k in range(1, spaces):
        share(k, place).wait_send()


def per_device(
    n, spaces, particle_amount, section_opacity, species_opacity_factor,
    absorber_molefraction, scaled_heat_level, wall_touching_flag, fraction_polynomial,
):
    sections, x_rows, ny, nz = particle_amount.shape
    gases = section_opacity.shape[1]
    per_gas = gases // n
    bits = n.bit_length() - 1
    slabs = x_rows // SLAB_ROWS
    rows = x_rows + 2 * HALO
    slab_rows = x_rows // slabs
    field = pltpu.VMEM((per_gas, rows, ny, nz), jnp.float32)
    dma = pltpu.SemaphoreType.DMA
    vmem, smem = pl.BlockSpec(memory_space=pltpu.VMEM), pl.BlockSpec(memory_space=pltpu.SMEM)
    divergence, average = pl.pallas_call(
        functools.partial(kernel, n, spaces, slabs, nz),
        out_shape=(
            jax.ShapeDtypeStruct((x_rows, ny, nz), jnp.float32),
            jax.ShapeDtypeStruct((1, 1), jnp.float32),
        ),
        in_specs=[vmem, pl.BlockSpec(memory_space=pl.ANY), smem, vmem, vmem, vmem, smem],
        out_specs=(vmem, smem),
        scratch_shapes=[
            pltpu.VMEM((slabs, sections, slab_rows, ny, nz), jnp.bfloat16),
            pltpu.VMEM((slabs, n, per_gas, slab_rows, ny, nz), jnp.float32),
            [
                pltpu.VMEM((slabs, n >> (stage + 1), per_gas, slab_rows, ny, nz), jnp.float32)
                for stage in range(bits)
            ],
            field,
            pltpu.VMEM((rows, ny, nz), jnp.float32),
            pltpu.VMEM((rows, ny, nz), jnp.float32),
            field, field, field, field, field, field,
            pltpu.VMEM((2, per_gas, rows, ny, nz), jnp.float32),
            pltpu.VMEM((n, x_rows // n, ny, nz), jnp.float32),
            pltpu.VMEM((spaces, ny, nz), jnp.float32),
            pltpu.VMEM((n, ny, nz), jnp.float32),
            pltpu.VMEM((x_rows, ny, nz), jnp.float32),
            pltpu.VMEM((gases * ny, sections * ny), jnp.bfloat16),
            dma((slabs,)), dma((bits, slabs)), dma((bits, slabs)), dma((3, 2)), dma((3, 2)),
            dma((n,)), dma((n,)), dma((n,)), dma((n,)), dma((spaces,)), dma((spaces,)),
            dma((n,)), dma((n,)),
        ],
        compiler_params=pltpu.CompilerParams(
            collective_id=0, has_side_effects=True, vmem_limit_bytes=56 * 1024 * 1024
        ),
    )(
        section_opacity.T, particle_amount, species_opacity_factor, absorber_molefraction,
        scaled_heat_level, wall_touching_flag, fraction_polynomial.T,
    )
    return divergence, average.reshape(())


def solution(mesh):
    return jax.shard_map(
        functools.partial(per_device, mesh.shape["gas"], mesh.shape["space"]),
        mesh=mesh,
        in_specs=(
            P("gas", "space", None, None),
            P("gas", None),
            P(),
            P("space", None, None),
            P("space", None, None),
            P("space", None, None),
            P(),
        ),
        out_specs=(P("space", None, None), P()),
        check_vma=False,
    )
```

```python
import functools

import jax
import jax.numpy as jnp
from jax import lax
from jax.experimental import pallas as pl
from jax.experimental.pallas import tpu as pltpu
from jax.sharding import PartitionSpec as P

SWEEPS = 6
HALO = SWEEPS - 1
BLOCK = 8
AHEAD = 3
SLAB_ROWS = 8
Z_FIRST = (1,)
KAPPA_FLOOR = 0.5
WALL_LOSS = 0.5
LAM_LOW = 0.5
LAM_HIGH = 12.0
CENTRE = (LAM_HIGH + LAM_LOW) / 2.0
SPREAD = (LAM_HIGH - LAM_LOW) / 2.0
MESH = pl.DeviceIdType.MESH


def coupling(total):
    positive = total > 0.0
    return jnp.where(positive, 2.0 / (3.0 * jnp.where(positive, total, 1.0)), 0.0)


def kernel(
    n, spaces, slabs, cells,
    opacity_t, amount, strength, mole, heat, flag, poly,
    out, average,
    amount_v, acc, recvs, absorb, heat_w, wall_w, cx, cy, cz, diag, res, rem, dirs,
    parts, totals, gas_totals, mine, kron,
    load_sem, rs_send, rs_recv, halo_send, halo_recv, sum_send, sum_recv,
    gather_send, gather_recv, total_send, total_recv, greet_send, greet_recv,
):
    bits = n.bit_length() - 1
    me, place = lax.axis_index("gas"), lax.axis_index("space")
    per_gas = acc.shape[2]
    x_rows, rows = heat.shape[0], heat_w.shape[0]
    slab_rows = x_rows // slabs
    edge = -(-HALO // slab_rows)
    order = (
        list(range(edge)) + list(range(slabs - edge, slabs)) + list(range(edge, slabs - edge))
    )
    low_first = list(range(bits))
    high_first = low_first[1:] + low_first[:1]
    bit_order = {
        slab: high_first if at % 8 in Z_FIRST else low_first for at, slab in enumerate(order)
    }

    def load(slab):
        return pltpu.make_async_copy(
            amount.at[:, pl.ds(slab * slab_rows, slab_rows)], amount_v.at[slab], load_sem.at[slab]
        )

    for slab in order[:AHEAD]:
        load(slab).start()

    barrier = pltpu.get_barrier_semaphore()
    for k in range(1, n):
        pl.semaphore_signal(
            barrier, inc=1, device_id={"gas": lax.rem(me + k, n)}, device_id_type=MESH
        )
    for k in range(1, spaces):
        pl.semaphore_signal(
            barrier, inc=1, device_id={"space": lax.rem(place + k, spaces)}, device_id_type=MESH
        )
    heat_w[HALO : HALO + x_rows] = heat[...]
    wall_w[HALO : HALO + x_rows] = WALL_LOSS * flag[...].astype(jnp.float32)
    gases, sections = opacity_t.shape
    ny = heat.shape[1]
    line = lax.broadcasted_iota(jnp.int32, (gases * ny, gases), 0) // ny
    picks = line == lax.broadcasted_iota(jnp.int32, (gases * ny, gases), 1)
    spread = lax.broadcasted_iota(jnp.int32, (sections, sections * ny), 1) // ny
    widens = spread == lax.broadcasted_iota(jnp.int32, (sections, sections * ny), 0)
    rows_of = jnp.dot(
        jnp.where(picks, 1.0, 0.0).astype(jnp.bfloat16), opacity_t[...],
        preferred_element_type=jnp.float32,
    ).astype(jnp.bfloat16)
    wide = jnp.dot(
        rows_of, jnp.where(widens, 1.0, 0.0).astype(jnp.bfloat16),
        preferred_element_type=jnp.float32,
    )
    same = (
        lax.broadcasted_iota(jnp.int32, wide.shape, 0) % ny
        == lax.broadcasted_iota(jnp.int32, wide.shape, 1) % ny
    )
    kron[...] = jnp.where(same, wide, 0.0).astype(jnp.bfloat16)
    pl.semaphore_wait(barrier, n - 1 + spaces - 1)

    right, left = lax.rem(place + 1, spaces), lax.rem(place + spaces - 1, spaces)

    def halo_pair(which, before, after, to_right, to_left):
        return [
            pltpu.make_async_remote_copy(
                src_ref=to_right, dst_ref=before,
                send_sem=halo_send.at[which, 0], recv_sem=halo_recv.at[which, 0],
                device_id={"space": right}, device_id_type=MESH,
            ),
            pltpu.make_async_remote_copy(
                src_ref=to_left, dst_ref=after,
                send_sem=halo_send.at[which, 1], recv_sem=halo_recv.at[which, 1],
                device_id={"space": left}, device_id_type=MESH,
            ),
        ]

    pairs = []
    for which, ref in enumerate((heat_w, wall_w)):
        pairs += halo_pair(
            which,
            ref.at[pl.ds(0, HALO)], ref.at[pl.ds(HALO + x_rows, HALO)],
            ref.at[pl.ds(x_rows, HALO)], ref.at[pl.ds(HALO, HALO)],
        )
    for copy in pairs:
        copy.start()

    def base(stage, slab):
        return sum(
            ((me >> bit) & 1) * (n >> (at + 1)) for at, bit in enumerate(bit_order[slab][:stage])
        ) + jnp.int32(0)

    def spot(owner, slab):
        return sum(
            ((owner >> bit) & 1) * (n >> (at + 1)) for at, bit in enumerate(bit_order[slab])
        )

    def exchange(stage, slab):
        half = n >> (stage + 1)
        level = bit_order[slab][stage]
        bit = (me >> level) & 1
        partner = me + (1 - 2 * bit) * (1 << level)
        return pltpu.make_async_remote_copy(
            src_ref=acc.at[slab, pl.ds(base(stage, slab) + (1 - bit) * half, half)],
            dst_ref=recvs[stage].at[slab],
            send_sem=rs_send.at[stage, slab], recv_sem=rs_recv.at[stage, slab],
            device_id={"gas": partner}, device_id_type=MESH,
        )

    def opacity(slab):
        load(slab).wait()

        def one(x, carry):
            column = amount_v[slab, :, x].reshape(-1, cells)
            value = jnp.dot(kron[...], column, preferred_element_type=jnp.float32)
            value = value.reshape((n, per_gas) + acc.shape[4:])
            for owner in range(n):
                acc[slab, spot(owner, slab), :, x] = value[owner]
            return carry

        lax.fori_loop(0, slab_rows, one, 0)

    absorb_pair = halo_pair(
        2,
        absorb.at[:, pl.ds(0, HALO)], absorb.at[:, pl.ds(HALO + x_rows, HALO)],
        absorb.at[:, pl.ds(x_rows, HALO)], absorb.at[:, pl.ds(HALO, HALO)],
    )

    for step in range(slabs + bits):
        if step < slabs:
            if step + AHEAD < slabs:
                load(order[step + AHEAD]).start()
            opacity(order[step])
            exchange(0, order[step]).start()
        for stage in range(bits):
            at = step - stage - 1
            if not 0 <= at < slabs:
                continue
            slab = order[at]
            exchange(stage, slab).wait_recv()
            if stage < bits - 1:
                half = n >> (stage + 1)
                kept = pl.ds(base(stage + 1, slab), half)
                acc[slab, kept] = acc[slab, kept] + recvs[stage][slab]
                exchange(stage + 1, slab).start()
            else:
                inner = pl.ds(slab * slab_rows, slab_rows)
                for i in range(per_gas):
                    absorb[i, pl.ds(HALO + slab * slab_rows, slab_rows)] = (
                        KAPPA_FLOOR + strength[me * per_gas + i] * mole[inner]
                        + (acc[slab, base(bits, slab), i] + recvs[stage][slab, 0, i])
                    )
                if at == 2 * edge - 1:
                    for copy in absorb_pair:
                        copy.start()

    for copy in pairs + absorb_pair:
        copy.wait()
    absorb[:, 0:HALO] = jnp.where(place == 0, 0.0, absorb[:, 0:HALO])
    absorb[:, HALO + x_rows :] = jnp.where(place == spaces - 1, 0.0, absorb[:, HALO + x_rows :])

    tile = heat.shape[1:]
    block = (BLOCK,) + tile
    y_at = lax.broadcasted_iota(jnp.int32, block, 1)
    z_at = lax.broadcasted_iota(jnp.int32, block, 2)
    y_low, y_top = y_at == 0, y_at == tile[0] - 1
    z_low, z_top = z_at == 0, z_at == tile[1] - 1

    def begin(i, at):
        level = heat_w[at]
        square = level * level
        gas = me * per_gas + i
        emitted = (poly[0, gas] + poly[1, gas] * level + poly[2, gas] * square) * (square * square)
        first = absorb[i, at] * emitted
        return emitted, first, first / CENTRE

    def put_begin(i, at, values):
        rem[i, at], res[i, at], dirs[0, i, at] = values

    def face(a, b):
        full = coupling(a + b)
        return full, jnp.where((a > 0.0) & (b > 0.0), full, 0.0)

    for i in range(per_gas):
        for at in (pl.ds(0, 1), pl.ds(rows - 1, 1)):
            put_begin(i, at, begin(i, at))
            dirs[1, i, at] = jnp.zeros((1,) + tile, jnp.float32)
        cx[i, rows - 1] = face(absorb[i, rows - 2], absorb[i, rows - 1])[1]

    def prepare(step, carry):
        row = 1 + step * BLOCK
        at = pl.ds(row, BLOCK)
        found = []
        for i in range(per_gas):
            around = absorb[i, pl.ds(row - 1, BLOCK + 2)]
            here = around[1:-1]
            full, off = face(around[:-1], around[1:])
            edge = coupling(here)
            y_face = coupling(here + pltpu.roll(here, 1, 1))
            z_face = coupling(here + pltpu.roll(here, 1, 2))
            y_up = jnp.where(y_top, edge, pltpu.roll(y_face, tile[0] - 1, 1))
            z_up = jnp.where(z_top, edge, pltpu.roll(z_face, tile[1] - 1, 2))
            middle = (
                here + wall_w[at] + full[:-1] + full[1:]
                + jnp.where(y_low, edge, y_face) + y_up
                + jnp.where(z_low, edge, z_face) + z_up
            )
            found.append((
                off[:-1], jnp.where(y_low, 0.0, y_face), jnp.where(z_low, 0.0, z_face), middle,
                begin(i, at),
            ))
        for i in range(per_gas):
            cx[i, at], cy[i, at], cz[i, at], diag[i, at], values = found[i]
            put_begin(i, at, values)
        return carry

    lax.fori_loop(0, (rows - 2) // BLOCK, prepare, 0)

    sigma = CENTRE / SPREAD
    ratio = 1.0 / sigma
    for sweep in range(SWEEPS - 1):
        following = 1.0 / (2.0 * sigma - ratio)
        keep, gain = following * ratio, 2.0 * following / SPREAD
        ratio = following
        source, target = sweep % 2, (sweep + 1) % 2
        skip = sweep * 2 // BLOCK * BLOCK // 2

        def relax(step, carry):
            row = 1 + skip + step * BLOCK
            at = pl.ds(row, BLOCK)
            found = []
            for i in range(per_gas):
                around = dirs[source, i, pl.ds(row - 1, BLOCK + 2)]
                d = around[1:-1]
                c_x, c_y, c_z = cx[i, pl.ds(row, BLOCK + 1)], cy[i, at], cz[i, at]
                applied = diag[i, at] * d
                applied -= c_x[:-1] * around[:-2]
                applied -= c_x[1:] * around[2:]
                applied -= c_y * pltpu.roll(d, 1, 1) + pltpu.roll(c_y * d, tile[0] - 1, 1)
                applied -= c_z * pltpu.roll(d, 1, 2) + pltpu.roll(c_z * d, tile[1] - 1, 2)
                left_over = res[i, at] - applied
                found.append((left_over, rem[i, at] - d, keep * d + gain * left_over))
            for i in range(per_gas):
                res[i, at], rem[i, at], dirs[target, i, at] = found[i]
            return carry

        lax.fori_loop(0, (rows - 2 - 2 * skip) // BLOCK, relax, 0)

    last = (SWEEPS - 1) % 2

    def finish(step, carry):
        at = pl.ds(HALO + step * BLOCK, BLOCK)
        total = absorb[0, at] * (rem[0, at] - dirs[last, 0, at])
        for i in range(1, per_gas):
            total += absorb[i, at] * (rem[i, at] - dirs[last, i, at])
        mine[pl.ds(step * BLOCK, BLOCK)] = total
        return carry + jnp.sum(total, axis=0)

    gas_totals[me] = lax.fori_loop(
        0, x_rows // BLOCK, finish, jnp.zeros(tile, jnp.float32)
    )

    chunk = x_rows // n
    own = pl.ds(me * chunk, chunk)
    sends = []
    for k in range(1, n):
        peer = lax.rem(me + k, n)
        sends.append(pltpu.make_async_remote_copy(
            src_ref=mine.at[pl.ds(peer * chunk, chunk)], dst_ref=parts.at[k],
            send_sem=sum_send.at[k], recv_sem=sum_recv.at[k],
            device_id={"gas": peer}, device_id_type=MESH,
        ))
    def greet(k, origin):
        return pltpu.make_async_remote_copy(
            src_ref=gas_totals.at[origin], dst_ref=gas_totals.at[origin],
            send_sem=greet_send.at[k], recv_sem=greet_recv.at[k],
            device_id={"gas": lax.rem(me + k, n)}, device_id_type=MESH,
        )

    for k in range(1, n):
        greet(k, me).start()
    for copy in sends:
        copy.start()
    total = mine[own]
    for k in range(1, n):
        sends[k - 1].wait_recv()
        total = total + parts[k]
    out[own] = total

    def gather(k, origin):
        held = pl.ds(origin * chunk, chunk)
        return pltpu.make_async_remote_copy(
            src_ref=out.at[held], dst_ref=out.at[held],
            send_sem=gather_send.at[k], recv_sem=gather_recv.at[k],
            device_id={"gas": lax.rem(me + k, n)}, device_id_type=MESH,
        )

    for k in range(1, n):
        gather(k, me).start()
    for k in range(1, n):
        greet(k, lax.rem(me + n - k, n)).wait_recv()
    totals[place] = jnp.sum(gas_totals[...], axis=0)

    def share(k, origin):
        return pltpu.make_async_remote_copy(
            src_ref=totals.at[origin], dst_ref=totals.at[origin],
            send_sem=total_send.at[k], recv_sem=total_recv.at[k],
            device_id={"space": lax.rem(place + k, spaces)}, device_id_type=MESH,
        )

    for k in range(1, spaces):
        share(k, place).start()
    for k in range(1, spaces):
        share(k, lax.rem(place + spaces - k, spaces)).wait_recv()
    for k in range(1, n):
        gather(k, lax.rem(me + n - k, n)).wait_recv()
    whole = jnp.sum(jnp.sum(totals[...], axis=0))
    average[0, 0] = whole * (1.0 / (x_rows * spaces * tile[0] * tile[1]))

    for stage in range(bits):
        for slab in range(slabs):
            exchange(stage, slab).wait_send()
    for k in range(1, n):
        sends[k - 1].wait_send()
        gather(k, me).wait_send()
        greet(k, me).wait_send()
    for k in range(1, spaces):
        share(k, place).wait_send()


def per_device(
    n, spaces, particle_amount, section_opacity, species_opacity_factor,
    absorber_molefraction, scaled_heat_level, wall_touching_flag, fraction_polynomial,
):
    sections, x_rows, ny, nz = particle_amount.shape
    gases = section_opacity.shape[1]
    per_gas = gases // n
    bits = n.bit_length() - 1
    slabs = x_rows // SLAB_ROWS
    rows = x_rows + 2 * HALO
    slab_rows = x_rows // slabs
    field = pltpu.VMEM((per_gas, rows, ny, nz), jnp.float32)
    dma = pltpu.SemaphoreType.DMA
    vmem, smem = pl.BlockSpec(memory_space=pltpu.VMEM), pl.BlockSpec(memory_space=pltpu.SMEM)
    divergence, average = pl.pallas_call(
        functools.partial(kernel, n, spaces, slabs, nz),
        out_shape=(
            jax.ShapeDtypeStruct((x_rows, ny, nz), jnp.float32),
            jax.ShapeDtypeStruct((1, 1), jnp.float32),
        ),
        in_specs=[vmem, pl.BlockSpec(memory_space=pl.ANY), smem, vmem, vmem, vmem, smem],
        out_specs=(vmem, smem),
        scratch_shapes=[
            pltpu.VMEM((slabs, sections, slab_rows, ny, nz), jnp.bfloat16),
            pltpu.VMEM((slabs, n, per_gas, slab_rows, ny, nz), jnp.float32),
            [
                pltpu.VMEM((slabs, n >> (stage + 1), per_gas, slab_rows, ny, nz), jnp.float32)
                for stage in range(bits)
            ],
            field,
            pltpu.VMEM((rows, ny, nz), jnp.float32),
            pltpu.VMEM((rows, ny, nz), jnp.float32),
            field, field, field, field, field, field,
            pltpu.VMEM((2, per_gas, rows, ny, nz), jnp.float32),
            pltpu.VMEM((n, x_rows // n, ny, nz), jnp.float32),
            pltpu.VMEM((spaces, ny, nz), jnp.float32),
            pltpu.VMEM((n, ny, nz), jnp.float32),
            pltpu.VMEM((x_rows, ny, nz), jnp.float32),
            pltpu.VMEM((gases * ny, sections * ny), jnp.bfloat16),
            dma((slabs,)), dma((bits, slabs)), dma((bits, slabs)), dma((3, 2)), dma((3, 2)),
            dma((n,)), dma((n,)), dma((n,)), dma((n,)), dma((spaces,)), dma((spaces,)),
            dma((n,)), dma((n,)),
        ],
        compiler_params=pltpu.CompilerParams(
            collective_id=0, has_side_effects=True, vmem_limit_bytes=56 * 1024 * 1024
        ),
    )(
        section_opacity.T, particle_amount, species_opacity_factor, absorber_molefraction,
        scaled_heat_level, wall_touching_flag, fraction_polynomial.T,
    )
    return divergence, average.reshape(())


def solution(mesh):
    return jax.shard_map(
        functools.partial(per_device, mesh.shape["gas"], mesh.shape["space"]),
        mesh=mesh,
        in_specs=(
            P("gas", "space", None, None),
            P("gas", None),
            P(),
            P("space", None, None),
            P("space", None, None),
            P("space", None, None),
            P(),
        ),
        out_specs=(P("space", None, None), P()),
        check_vma=False,
    )
```

```python
import functools

import jax
import jax.numpy as jnp
from jax import lax
from jax.experimental import pallas as pl
from jax.experimental.pallas import tpu as pltpu
from jax.sharding import PartitionSpec as P

SWEEPS = 6
HALO = SWEEPS - 1
BLOCK = 8
AHEAD = 3
SLAB_ROWS = 8
Z_FIRST = (1,)
KAPPA_FLOOR = 0.5
WALL_LOSS = 0.5
LAM_LOW = 0.5
LAM_HIGH = 12.0
CENTRE = (LAM_HIGH + LAM_LOW) / 2.0
SPREAD = (LAM_HIGH - LAM_LOW) / 2.0
MESH = pl.DeviceIdType.MESH


def coupling(total):
    positive = total > 0.0
    return jnp.where(positive, 2.0 / (3.0 * jnp.where(positive, total, 1.0)), 0.0)


def kernel(
    n, spaces, slabs, cells,
    opacity_t, amount, strength, mole, heat, flag, poly,
    out, average,
    amount_v, acc, recvs, absorb, heat_w, wall_w, cx, cy, cz, diag, res, rem, dirs,
    parts, totals, gas_totals, mine, kron,
    load_sem, rs_send, rs_recv, halo_send, halo_recv, sum_send, sum_recv,
    gather_send, gather_recv, total_send, total_recv, greet_send, greet_recv,
):
    bits = n.bit_length() - 1
    me, place = lax.axis_index("gas"), lax.axis_index("space")
    per_gas = acc.shape[2]
    x_rows, rows = heat.shape[0], heat_w.shape[0]
    slab_rows = x_rows // slabs
    edge = -(-HALO // slab_rows)
    order = (
        list(range(edge)) + list(range(slabs - edge, slabs)) + list(range(edge, slabs - edge))
    )
    low_first = list(range(bits))
    high_first = low_first[1:] + low_first[:1]
    bit_order = {
        slab: high_first if at % 8 in Z_FIRST else low_first for at, slab in enumerate(order)
    }

    def load(slab):
        return pltpu.make_async_copy(
            amount.at[:, pl.ds(slab * slab_rows, slab_rows)], amount_v.at[slab], load_sem.at[slab]
        )

    for slab in order[:AHEAD]:
        load(slab).start()

    barrier = pltpu.get_barrier_semaphore()
    for k in range(1, n):
        pl.semaphore_signal(
            barrier, inc=1, device_id={"gas": lax.rem(me + k, n)}, device_id_type=MESH
        )
    for k in range(1, spaces):
        pl.semaphore_signal(
            barrier, inc=1, device_id={"space": lax.rem(place + k, spaces)}, device_id_type=MESH
        )
    heat_w[HALO : HALO + x_rows] = heat[...]
    wall_w[HALO : HALO + x_rows] = WALL_LOSS * flag[...].astype(jnp.float32)
    gases, sections = opacity_t.shape
    ny = heat.shape[1]
    line = lax.broadcasted_iota(jnp.int32, (gases * ny, gases), 0) // ny
    picks = line == lax.broadcasted_iota(jnp.int32, (gases * ny, gases), 1)
    spread = lax.broadcasted_iota(jnp.int32, (sections, sections * ny), 1) // ny
    widens = spread == lax.broadcasted_iota(jnp.int32, (sections, sections * ny), 0)
    rows_of = jnp.dot(
        jnp.where(picks, 1.0, 0.0).astype(jnp.bfloat16), opacity_t[...],
        preferred_element_type=jnp.float32,
    ).astype(jnp.bfloat16)
    wide = jnp.dot(
        rows_of, jnp.where(widens, 1.0, 0.0).astype(jnp.bfloat16),
        preferred_element_type=jnp.float32,
    )
    same = (
        lax.broadcasted_iota(jnp.int32, wide.shape, 0) % ny
        == lax.broadcasted_iota(jnp.int32, wide.shape, 1) % ny
    )
    kron[...] = jnp.where(same, wide, 0.0).astype(jnp.bfloat16)
    pl.semaphore_wait(barrier, n - 1 + spaces - 1)

    right, left = lax.rem(place + 1, spaces), lax.rem(place + spaces - 1, spaces)

    def halo_pair(which, before, after, to_right, to_left):
        return [
            pltpu.make_async_remote_copy(
                src_ref=to_right, dst_ref=before,
                send_sem=halo_send.at[which, 0], recv_sem=halo_recv.at[which, 0],
                device_id={"space": right}, device_id_type=MESH,
            ),
            pltpu.make_async_remote_copy(
                src_ref=to_left, dst_ref=after,
                send_sem=halo_send.at[which, 1], recv_sem=halo_recv.at[which, 1],
                device_id={"space": left}, device_id_type=MESH,
            ),
        ]

    pairs = []
    for which, ref in enumerate((heat_w, wall_w)):
        pairs += halo_pair(
            which,
            ref.at[pl.ds(0, HALO)], ref.at[pl.ds(HALO + x_rows, HALO)],
            ref.at[pl.ds(x_rows, HALO)], ref.at[pl.ds(HALO, HALO)],
        )
    for copy in pairs:
        copy.start()

    def base(stage, slab):
        return sum(
            ((me >> bit) & 1) * (n >> (at + 1)) for at, bit in enumerate(bit_order[slab][:stage])
        ) + jnp.int32(0)

    def spot(owner, slab):
        return sum(
            ((owner >> bit) & 1) * (n >> (at + 1)) for at, bit in enumerate(bit_order[slab])
        )

    def exchange(stage, slab):
        half = n >> (stage + 1)
        level = bit_order[slab][stage]
        bit = (me >> level) & 1
        partner = me + (1 - 2 * bit) * (1 << level)
        return pltpu.make_async_remote_copy(
            src_ref=acc.at[slab, pl.ds(base(stage, slab) + (1 - bit) * half, half)],
            dst_ref=recvs[stage].at[slab],
            send_sem=rs_send.at[stage, slab], recv_sem=rs_recv.at[stage, slab],
            device_id={"gas": partner}, device_id_type=MESH,
        )

    def opacity(slab):
        load(slab).wait()

        def one(x, carry):
            column = amount_v[slab, :, x].reshape(-1, cells)
            value = jnp.dot(kron[...], column, preferred_element_type=jnp.float32)
            value = value.reshape((n, per_gas) + acc.shape[4:])
            for owner in range(n):
                acc[slab, spot(owner, slab), :, x] = value[owner]
            return carry

        lax.fori_loop(0, slab_rows, one, 0)

    absorb_pair = halo_pair(
        2,
        absorb.at[:, pl.ds(0, HALO)], absorb.at[:, pl.ds(HALO + x_rows, HALO)],
        absorb.at[:, pl.ds(x_rows, HALO)], absorb.at[:, pl.ds(HALO, HALO)],
    )

    for step in range(slabs + bits):
        if step < slabs:
            if step + AHEAD < slabs:
                load(order[step + AHEAD]).start()
            opacity(order[step])
            exchange(0, order[step]).start()
        for stage in reversed(range(bits)):
            at = step - stage - 1
            if not 0 <= at < slabs:
                continue
            slab = order[at]
            exchange(stage, slab).wait_recv()
            if stage < bits - 1:
                half = n >> (stage + 1)
                kept = pl.ds(base(stage + 1, slab), half)
                acc[slab, kept] = acc[slab, kept] + recvs[stage][slab]
                exchange(stage + 1, slab).start()
            else:
                inner = pl.ds(slab * slab_rows, slab_rows)
                for i in range(per_gas):
                    absorb[i, pl.ds(HALO + slab * slab_rows, slab_rows)] = (
                        KAPPA_FLOOR + strength[me * per_gas + i] * mole[inner]
                        + (acc[slab, base(bits, slab), i] + recvs[stage][slab, 0, i])
                    )
                if at == 2 * edge - 1:
                    for copy in absorb_pair:
                        copy.start()

    for copy in pairs + absorb_pair:
        copy.wait()
    absorb[:, 0:HALO] = jnp.where(place == 0, 0.0, absorb[:, 0:HALO])
    absorb[:, HALO + x_rows :] = jnp.where(place == spaces - 1, 0.0, absorb[:, HALO + x_rows :])

    tile = heat.shape[1:]
    block = (BLOCK,) + tile
    y_at = lax.broadcasted_iota(jnp.int32, block, 1)
    z_at = lax.broadcasted_iota(jnp.int32, block, 2)
    y_low, y_top = y_at == 0, y_at == tile[0] - 1
    z_low, z_top = z_at == 0, z_at == tile[1] - 1

    def begin(i, at):
        level = heat_w[at]
        square = level * level
        gas = me * per_gas + i
        emitted = (poly[0, gas] + poly[1, gas] * level + poly[2, gas] * square) * (square * square)
        first = absorb[i, at] * emitted
        return emitted, first, first / CENTRE

    def put_begin(i, at, values):
        rem[i, at], res[i, at], dirs[0, i, at] = values

    def face(a, b):
        full = coupling(a + b)
        return full, jnp.where((a > 0.0) & (b > 0.0), full, 0.0)

    for i in range(per_gas):
        for at in (pl.ds(0, 1), pl.ds(rows - 1, 1)):
            put_begin(i, at, begin(i, at))
            dirs[1, i, at] = jnp.zeros((1,) + tile, jnp.float32)
        cx[i, rows - 1] = face(absorb[i, rows - 2], absorb[i, rows - 1])[1]

    def prepare(step, carry):
        row = 1 + step * BLOCK
        at = pl.ds(row, BLOCK)
        found = []
        for i in range(per_gas):
            around = absorb[i, pl.ds(row - 1, BLOCK + 2)]
            here = around[1:-1]
            full, off = face(around[:-1], around[1:])
            edge = coupling(here)
            y_face = coupling(here + pltpu.roll(here, 1, 1))
            z_face = coupling(here + pltpu.roll(here, 1, 2))
            y_up = jnp.where(y_top, edge, pltpu.roll(y_face, tile[0] - 1, 1))
            z_up = jnp.where(z_top, edge, pltpu.roll(z_face, tile[1] - 1, 2))
            middle = (
                here + wall_w[at] + full[:-1] + full[1:]
                + jnp.where(y_low, edge, y_face) + y_up
                + jnp.where(z_low, edge, z_face) + z_up
            )
            found.append((
                off[:-1], jnp.where(y_low, 0.0, y_face), jnp.where(z_low, 0.0, z_face), middle,
                begin(i, at),
            ))
        for i in range(per_gas):
            cx[i, at], cy[i, at], cz[i, at], diag[i, at], values = found[i]
            put_begin(i, at, values)
        return carry

    lax.fori_loop(0, (rows - 2) // BLOCK, prepare, 0)

    sigma = CENTRE / SPREAD
    ratio = 1.0 / sigma
    for sweep in range(SWEEPS - 1):
        following = 1.0 / (2.0 * sigma - ratio)
        keep, gain = following * ratio, 2.0 * following / SPREAD
        ratio = following
        source, target = sweep % 2, (sweep + 1) % 2
        skip = sweep * 2 // BLOCK * BLOCK // 2

        def relax(step, carry):
            row = 1 + skip + step * BLOCK
            at = pl.ds(row, BLOCK)
            found = []
            for i in range(per_gas):
                around = dirs[source, i, pl.ds(row - 1, BLOCK + 2)]
                d = around[1:-1]
                c_x, c_y, c_z = cx[i, pl.ds(row, BLOCK + 1)], cy[i, at], cz[i, at]
                applied = diag[i, at] * d
                applied -= c_x[:-1] * around[:-2]
                applied -= c_x[1:] * around[2:]
                applied -= c_y * pltpu.roll(d, 1, 1) + pltpu.roll(c_y * d, tile[0] - 1, 1)
                applied -= c_z * pltpu.roll(d, 1, 2) + pltpu.roll(c_z * d, tile[1] - 1, 2)
                left_over = res[i, at] - applied
                found.append((left_over, rem[i, at] - d, keep * d + gain * left_over))
            for i in range(per_gas):
                res[i, at], rem[i, at], dirs[target, i, at] = found[i]
            return carry

        lax.fori_loop(0, (rows - 2 - 2 * skip) // BLOCK, relax, 0)

    last = (SWEEPS - 1) % 2

    def finish(step, carry):
        at = pl.ds(HALO + step * BLOCK, BLOCK)
        total = absorb[0, at] * (rem[0, at] - dirs[last, 0, at])
        for i in range(1, per_gas):
            total += absorb[i, at] * (rem[i, at] - dirs[last, i, at])
        mine[pl.ds(step * BLOCK, BLOCK)] = total
        return carry + jnp.sum(total, axis=0)

    gas_totals[me] = lax.fori_loop(
        0, x_rows // BLOCK, finish, jnp.zeros(tile, jnp.float32)
    )

    chunk = x_rows // n
    own = pl.ds(me * chunk, chunk)
    sends = []
    for k in range(1, n):
        peer = lax.rem(me + k, n)
        sends.append(pltpu.make_async_remote_copy(
            src_ref=mine.at[pl.ds(peer * chunk, chunk)], dst_ref=parts.at[k],
            send_sem=sum_send.at[k], recv_sem=sum_recv.at[k],
            device_id={"gas": peer}, device_id_type=MESH,
        ))
    def greet(k, origin):
        return pltpu.make_async_remote_copy(
            src_ref=gas_totals.at[origin], dst_ref=gas_totals.at[origin],
            send_sem=greet_send.at[k], recv_sem=greet_recv.at[k],
            device_id={"gas": lax.rem(me + k, n)}, device_id_type=MESH,
        )

    for k in range(1, n):
        greet(k, me).start()
    for copy in sends:
        copy.start()
    total = mine[own]
    for k in range(1, n):
        sends[k - 1].wait_recv()
        total = total + parts[k]
    out[own] = total

    def gather(k, origin):
        held = pl.ds(origin * chunk, chunk)
        return pltpu.make_async_remote_copy(
            src_ref=out.at[held], dst_ref=out.at[held],
            send_sem=gather_send.at[k], recv_sem=gather_recv.at[k],
            device_id={"gas": lax.rem(me + k, n)}, device_id_type=MESH,
        )

    for k in range(1, n):
        gather(k, me).start()
    for k in range(1, n):
        greet(k, lax.rem(me + n - k, n)).wait_recv()
    totals[place] = jnp.sum(gas_totals[...], axis=0)

    def share(k, origin):
        return pltpu.make_async_remote_copy(
            src_ref=totals.at[origin], dst_ref=totals.at[origin],
            send_sem=total_send.at[k], recv_sem=total_recv.at[k],
            device_id={"space": lax.rem(place + k, spaces)}, device_id_type=MESH,
        )

    for k in range(1, spaces):
        share(k, place).start()
    for k in range(1, spaces):
        share(k, lax.rem(place + spaces - k, spaces)).wait_recv()
    for k in range(1, n):
        gather(k, lax.rem(me + n - k, n)).wait_recv()
    whole = jnp.sum(jnp.sum(totals[...], axis=0))
    average[0, 0] = whole * (1.0 / (x_rows * spaces * tile[0] * tile[1]))

    for stage in range(bits):
        for slab in range(slabs):
            exchange(stage, slab).wait_send()
    for k in range(1, n):
        sends[k - 1].wait_send()
        gather(k, me).wait_send()
        greet(k, me).wait_send()
    for k in range(1, spaces):
        share(k, place).wait_send()


def per_device(
    n, spaces, particle_amount, section_opacity, species_opacity_factor,
    absorber_molefraction, scaled_heat_level, wall_touching_flag, fraction_polynomial,
):
    sections, x_rows, ny, nz = particle_amount.shape
    gases = section_opacity.shape[1]
    per_gas = gases // n
    bits = n.bit_length() - 1
    slabs = x_rows // SLAB_ROWS
    rows = x_rows + 2 * HALO
    slab_rows = x_rows // slabs
    field = pltpu.VMEM((per_gas, rows, ny, nz), jnp.float32)
    dma = pltpu.SemaphoreType.DMA
    vmem, smem = pl.BlockSpec(memory_space=pltpu.VMEM), pl.BlockSpec(memory_space=pltpu.SMEM)
    divergence, average = pl.pallas_call(
        functools.partial(kernel, n, spaces, slabs, nz),
        out_shape=(
            jax.ShapeDtypeStruct((x_rows, ny, nz), jnp.float32),
            jax.ShapeDtypeStruct((1, 1), jnp.float32),
        ),
        in_specs=[vmem, pl.BlockSpec(memory_space=pl.ANY), smem, vmem, vmem, vmem, smem],
        out_specs=(vmem, smem),
        scratch_shapes=[
            pltpu.VMEM((slabs, sections, slab_rows, ny, nz), jnp.bfloat16),
            pltpu.VMEM((slabs, n, per_gas, slab_rows, ny, nz), jnp.float32),
            [
                pltpu.VMEM((slabs, n >> (stage + 1), per_gas, slab_rows, ny, nz), jnp.float32)
                for stage in range(bits)
            ],
            field,
            pltpu.VMEM((rows, ny, nz), jnp.float32),
            pltpu.VMEM((rows, ny, nz), jnp.float32),
            field, field, field, field, field, field,
            pltpu.VMEM((2, per_gas, rows, ny, nz), jnp.float32),
            pltpu.VMEM((n, x_rows // n, ny, nz), jnp.float32),
            pltpu.VMEM((spaces, ny, nz), jnp.float32),
            pltpu.VMEM((n, ny, nz), jnp.float32),
            pltpu.VMEM((x_rows, ny, nz), jnp.float32),
            pltpu.VMEM((gases * ny, sections * ny), jnp.bfloat16),
            dma((slabs,)), dma((bits, slabs)), dma((bits, slabs)), dma((3, 2)), dma((3, 2)),
            dma((n,)), dma((n,)), dma((n,)), dma((n,)), dma((spaces,)), dma((spaces,)),
            dma((n,)), dma((n,)),
        ],
        compiler_params=pltpu.CompilerParams(
            collective_id=0, has_side_effects=True, vmem_limit_bytes=56 * 1024 * 1024
        ),
    )(
        section_opacity.T, particle_amount, species_opacity_factor, absorber_molefraction,
        scaled_heat_level, wall_touching_flag, fraction_polynomial.T,
    )
    return divergence, average.reshape(())


def solution(mesh):
    return jax.shard_map(
        functools.partial(per_device, mesh.shape["gas"], mesh.shape["space"]),
        mesh=mesh,
        in_specs=(
            P("gas", "space", None, None),
            P("gas", None),
            P(),
            P("space", None, None),
            P("space", None, None),
            P("space", None, None),
            P(),
        ),
        out_specs=(P("space", None, None), P()),
        check_vma=False,
    )
```
